32 devices in a mesh: grp: 2 (over y), tok: 4 (over z), tp: 4 (over x, core).
Axes of the slice: x: 2, y: 2, z: 4, core: 2. Of those that a mesh axis runs over, the one named last changes fastest.
Arguments:
- inputs: bfloat16 [256, 8192], P(('grp', 'tok'), 'tp'), parts along dimension 0, may hold values from -6 to 6
- gate_weight: bfloat16 [8192, 16384], P('tp', 'tok'), may hold values from -0.0625 to 0.0625
- up_weight: bfloat16 [8192, 16384], P('tp', 'tok'), may hold values from -0.0625 to 0.0625
- down_weight: bfloat16 [16384, 4096], P('tok', 'tp'), may hold values from -0.046875 to 0.046875
Outputs:
- gram: float32 [8192, 4096], P(('grp', 'tok'), 'tp'), parts along dimension 0
- cross: float32 [8192, 4096], P(('grp', 'tok'), 'tp'), parts along dimension 0
The draws below stay inside these ranges and needn't reach their ends.
There are 2 independent parts, one for each index of `grp`. The reference program is written for one: setup_inputs(seed, part) draws one part's arguments, and reference() takes and returns one part's arrays. A program takes and returns all parts, laid end to end along the dimension named above; an argument that names none is the same for every part. Nothing has to cross between parts.
All inputs are finite; a program needn't handle non-finite values.
Results may differ from the reference program's by a relative error of at most 0.02.
Values may be sent and summed in bfloat16 or wider, within the bound.
A program may use at most 192 MiB of HBM per device.

```python
import jax
import jax.numpy as jnp
from jax import lax

D = 8192
FFW = 16384
WIN = 4096
TGT = 4096
TOK_DEV = 32
TOKENS = 128
N_TOK = 4
N_TP = 4


def block_levels(key, shape, shards, low, high):
    gain, own = 1.0, jax.random.fold_in(key, 6)
    for position, blocks in shards:
        heights = jnp.exp(jax.random.uniform(jax.random.fold_in(own, position), (blocks,), jnp.float32, low / len(shards), high / len(shards)))
        gain = gain * jnp.repeat(heights, shape[position] // blocks).reshape([-1 if axis == position else 1 for axis in range(len(shape))])
    return gain


def bell_draw(stream_key, shape, scale, reach, pieces=(), dtype=jnp.bfloat16):
    entries = scale * jax.random.normal(stream_key, shape, jnp.float32)
    if pieces:
        entries = entries * block_levels(stream_key, shape, pieces, -0.22, 0.18)
    return jnp.clip(entries, -reach, reach).astype(dtype)


def setup_inputs(seed: int = 0, part: int = 0) -> dict:
    splits = jax.random.split(jax.random.key(seed), 5)
    own_keys = jax.random.split(jax.random.fold_in(splits[4], part), 5)
    return {
        "inputs": bell_draw(own_keys[0], (TOKENS, D), 1.0, 6.0, ((0, 4), (1, 4))),
        "gate_weight": bell_draw(splits[1], (D, FFW), D ** -0.5, 0.0625, ((0, 4), (1, 4))),
        "up_weight": bell_draw(splits[2], (D, FFW), D ** -0.5, 0.0625, ((0, 4), (1, 4))),
        "down_weight": bell_draw(splits[3], (FFW, TGT), FFW ** -0.5, 0.046875, ((0, 4), (1, 4))),
    }


def reference(inputs, gate_weight, up_weight, down_weight):
    shares = D // N_TP
    input_groups = inputs.reshape(TOKENS, N_TP, shares).transpose(1, 0, 2)
    gate_groups = gate_weight.reshape(N_TP, shares, FFW)
    up_groups = up_weight.reshape(N_TP, shares, FFW)

    def add_group(carry, trio):
        rows, gate_rows, up_rows = trio
        gate_part = jnp.dot(rows, gate_rows, preferred_element_type=jnp.float32).astype(jnp.bfloat16)
        up_part = jnp.dot(rows, up_rows, preferred_element_type=jnp.float32).astype(jnp.bfloat16)
        gate_part, up_part = lax.optimization_barrier((gate_part, up_part))
        return (carry[0] + gate_part.astype(jnp.float32), carry[1] + up_part.astype(jnp.float32)), None

    begin = (jnp.zeros((TOKENS, FFW), jnp.float32), jnp.zeros((TOKENS, FFW), jnp.float32))
    sums, unused = lax.scan(add_group, begin, (input_groups, gate_groups, up_groups))
    hidden = (jax.nn.silu(sums[0]) * sums[1]).astype(jnp.bfloat16)
    target = jnp.dot(hidden, down_weight, preferred_element_type=jnp.float32).astype(jnp.bfloat16)
    window = inputs[:, :WIN].reshape(N_TOK, TOK_DEV, WIN)
    blocks = target.reshape(N_TOK, TOK_DEV, TGT)

    def accumulate(carry, pair):
        win_block, tgt_block = pair
        gram_part = jnp.dot(win_block.T, win_block, preferred_element_type=jnp.float32).astype(jnp.bfloat16)
        cross_part = jnp.dot(win_block.T, tgt_block, preferred_element_type=jnp.float32).astype(jnp.bfloat16)
        gram_part, cross_part = lax.optimization_barrier((gram_part, cross_part))
        return (carry[0] + gram_part.astype(jnp.float32), carry[1] + cross_part.astype(jnp.float32)), None

    start = (jnp.zeros((WIN, WIN), jnp.float32), jnp.zeros((WIN, TGT), jnp.float32))
    totals, unused = lax.scan(accumulate, start, (window, blocks))
    return totals[0], totals[1]
```

```python
import functools

import jax
import jax.numpy as jnp
from jax import lax
from jax.experimental import pallas as pl
from jax.experimental.pallas import tpu as pltpu
from jax.sharding import PartitionSpec as P

WIN = 4096
CHUNK = 512
MESH = pl.DeviceIdType.MESH
F32 = jnp.float32
BF16 = jnp.bfloat16


def span_kernel(
    n_tok, n_tp,
    x_ref, gate_ref, up_ref, down_ref,
    tgt_ref, wrow_ref, wcol_ref,
    xg, wg, wd, part, r1, s1, r2, hid, acc, ts, tr, tg, wr, wc,
    ld_x, ld_w, ld_d, gs, gr, c1s, c1r, x1s, x1r, x2s, x2r, c2s, c2r,
    zs, zr, bs, br, wrs, wrr, wcs, wcr,
):
    t = lax.axis_index("tok")
    p = lax.axis_index("tp")
    core = lax.rem(p, 2)
    x = p // 2
    n_x = n_tp // 2
    nc, _, feats, w = wg.shape
    rows = xg.shape[1]
    m = n_tok * rows
    b = m // n_tp
    win_rows, win_cols = wr.shape[2], wc.shape[2]

    def tok_peer(k):
        return lax.rem(t + k, n_tok)

    def x_peer(k):
        return lax.rem(x + k, n_x)

    def remote(src, dst, ssem, rsem, **where):
        return pltpu.make_async_remote_copy(
            src_ref=src, dst_ref=dst, send_sem=ssem, recv_sem=rsem,
            device_id=where, device_id_type=MESH,
        )

    partner = p + 1 - 2 * core

    own_x = pltpu.make_async_copy(x_ref, xg.at[t], ld_x)
    own_x.start()

    def load_w(c, j):
        src = (gate_ref, up_ref)[j]
        cols = pl.ds(pl.multiple_of(c * w, w), w)
        return pltpu.make_async_copy(src.at[:, cols], wg.at[c, j], ld_w.at[c, j])

    def load_d(c):
        return pltpu.make_async_copy(
            down_ref.at[pl.ds(pl.multiple_of(c * w, w), w), :], wd.at[c], ld_d.at[c]
        )

    @pl.loop(0, nc)
    def _(c):
        load_w(c, 0).start()
        load_w(c, 1).start()

    @pl.loop(0, nc)
    def _(c):
        load_d(c).start()

    barrier = pltpu.get_barrier_semaphore()
    for k in range(1, n_tok):
        pl.semaphore_signal(barrier, inc=1, device_id={"tok": tok_peer(k)}, device_id_type=MESH)
    for k in range(1, n_tp):
        pl.semaphore_signal(barrier, inc=1, device_id={"tp": lax.rem(p + k, n_tp)}, device_id_type=MESH)
    pl.semaphore_wait(barrier, n_tok + n_tp - 2)

    def gather(k):
        to = tok_peer(k)
        return remote(x_ref, xg.at[t], gs.at[to], gr.at[t], tok=to)

    def gathered(k):
        src = tok_peer(k)
        return remote(x_ref, xg.at[src], gs.at[src], gr.at[src], tok=src)

    for k in range(1, n_tok):
        gather(k).start()
    own_x.wait()
    for k in range(1, n_tok):
        gathered(k).wait_recv()

    def core_sum(c):
        return remote(part.at[c, 1 - core], r1.at[c], c1s.at[c], c1r.at[c], tp=partner)

    def x_sum(c, k):
        to = x_peer(k)
        return remote(s1.at[c, to], r2.at[c, x], x1s.at[c, to], x1r.at[c, x], tp=2 * to + core)

    def x_summed(c, k):
        src = x_peer(k)
        return remote(s1.at[c, src], r2.at[c, src], x1s.at[c, src], x1r.at[c, src], tp=2 * src + core)

    def x_hid(c, k):
        to = x_peer(k)
        mine = hid.at[c, core * n_x + x]
        return remote(mine, mine, x2s.at[c, to], x2r.at[c, x], tp=2 * to + core)

    def x_hidden(c, k):
        src = x_peer(k)
        theirs = hid.at[c, core * n_x + src]
        return remote(theirs, theirs, x2s.at[c, src], x2r.at[c, src], tp=2 * src + core)

    def core_hid(c, k):
        at = x_peer(k)
        block = hid.at[c, core * n_x + at]
        return remote(block, block, c2s.at[c, at], c2r.at[c, at], tp=partner)

    def core_hidden(c, k):
        at = x_peer(k)
        block = hid.at[c, (1 - core) * n_x + at]
        return remote(block, block, c2s.at[c, at], c2r.at[c, at], tp=partner)

    acc[...] = jnp.zeros_like(acc)

    def step(s, carry):
        @pl.when(s < nc)
        def _():
            c = s
            load_w(c, 0).wait()
            load_w(c, 1).wait()
            every = xg[...].reshape(m, feats)
            for j in range(2):
                y = jnp.dot(every, wg[c, j], preferred_element_type=F32).astype(BF16)
                part[c, 0, j] = y[: m // 2]
                part[c, 1, j] = y[m // 2 :]
            core_sum(c).start()

        @pl.when((s >= 1) & (s < nc + 1))
        def _():
            c = s - 1
            core_sum(c).wait_recv()
            both = part[c, core].astype(F32) + r1[c].astype(F32)
            both = both.astype(BF16)
            for at in range(n_x):
                s1[c, at] = both[:, at * b : (at + 1) * b]
            for k in range(1, n_x):
                x_sum(c, k).start()

        @pl.when((s >= 3) & (s < nc + 3))
        def _():
            c = s - 3
            for k in range(1, n_x):
                x_summed(c, k).wait_recv()
            both = s1[c, x].astype(F32)
            for k in range(1, n_x):
                both = both + r2[c, x_peer(k)].astype(F32)
            g, u = both[0], both[1]
            hid[c, core * n_x + x] = (g / (1.0 + jnp.exp(-g)) * u).astype(BF16)
            for k in range(1, n_x):
                x_hid(c, k).start()
            core_hid(c, 0).start()

        @pl.when((s >= 4) & (s < nc + 4))
        def _():
            c = s - 4
            for k in range(1, n_x):
                x_hidden(c, k).wait_recv()
                core_hid(c, k).start()

        @pl.when(s >= 5)
        def _():
            c = s - 5
            for k in range(n_x):
                core_hidden(c, k).wait_recv()
            load_d(c).wait()
            acc[...] += jnp.dot(hid[c].reshape(m, w), wd[c], preferred_element_type=F32)

        return carry

    lax.fori_loop(0, nc + 5, step, 0)

    ts[...] = acc[...].astype(BF16).reshape(ts.shape)

    def z_sum(k):
        to = tok_peer(k)
        return remote(ts.at[to], tr.at[t], zs.at[to], zr.at[t], tok=to)

    def z_summed(k):
        src = tok_peer(k)
        return remote(ts.at[src], tr.at[src], zs.at[src], zr.at[src], tok=src)

    def z_all(k):
        to = tok_peer(k)
        return remote(tg.at[t], tg.at[t], bs.at[to], br.at[t], tok=to)

    def z_alled(k):
        src = tok_peer(k)
        return remote(tg.at[src], tg.at[src], bs.at[src], br.at[src], tok=src)

    for k in range(1, n_tok):
        z_sum(k).start()

    def col_copy(d):
        off = (d * win_cols) % feats
        return remote(xg.at[:, :, pl.ds(off, win_cols)], wc, wcs.at[d], wcr, tp=d)

    row_owner = (t * win_rows) // feats
    row_off = pl.multiple_of(lax.rem(t * win_rows, feats), win_rows)

    def row_copy(k):
        to = lax.rem(p + k, n_tp)
        return remote(xg.at[:, :, pl.ds(row_off, win_rows)], wr, wrs.at[k], wrr, tp=to)

    for d in range(n_tp):
        owner = d * win_cols // feats

        @pl.when(p == owner)
        def _(d=d, owner=owner):
            if d == owner:
                off = (d * win_cols) % feats
                wc[...] = xg[:, :, off : off + win_cols]
            else:
                col_copy(d).start()

    @pl.when(p == row_owner)
    def _():
        for k in range(1, n_tp):
            row_copy(k).start()
        wr[...] = xg[:, :, pl.ds(row_off, win_rows)]

    total = acc[pl.ds(pl.multiple_of(t * rows, rows), rows), :]
    for k in range(1, n_tok):
        z_summed(k).wait_recv()
        total = total + tr[tok_peer(k)].astype(F32)
    tg[t] = total.astype(BF16)
    for k in range(1, n_tok):
        z_all(k).start()

    @pl.when((p * win_cols) // feats != p)
    def _():
        col_copy(0).wait_recv()

    @pl.when(p != row_owner)
    def _():
        row_copy(1).wait_recv()

    wrow_ref[...] = wr[...].reshape(wrow_ref.shape)
    wcol_ref[...] = wc[...].reshape(wcol_ref.shape)
    for k in range(1, n_tok):
        z_alled(k).wait_recv()
    tgt_ref[...] = tg[...].reshape(tgt_ref.shape)

    @pl.loop(0, nc)
    def _(c):
        core_sum(c).wait_send()
        core_hid(c, 0).wait_send()
        for k in range(1, n_x):
            x_sum(c, k).wait_send()
            x_hid(c, k).wait_send()
            core_hid(c, k).wait_send()

    for k in range(1, n_tok):
        gather(k).wait_send()
        z_sum(k).wait_send()
        z_all(k).wait_send()
    for d in range(n_tp):
        owner = d * win_cols // feats
        if d != owner:

            @pl.when(p == owner)
            def _(d=d):
                col_copy(d).wait_send()

    @pl.when(p == row_owner)
    def _():
        for k in range(1, n_tp):
            row_copy(k).wait_send()


def span(inputs, gate_weight, up_weight, down_weight, n_tok, n_tp):
    rows, feats = inputs.shape
    half = gate_weight.shape[1]
    outs = down_weight.shape[1]
    m = n_tok * rows
    w = min(CHUNK, half)
    nc = half // w
    n_x = n_tp // 2
    b = m // n_tp
    win_rows, win_cols = WIN // n_tok, WIN // n_tp
    dma = pltpu.SemaphoreType.DMA
    anywhere = pl.BlockSpec(memory_space=pl.ANY)
    vmem = pl.BlockSpec(memory_space=pltpu.VMEM)
    return pl.pallas_call(
        functools.partial(span_kernel, n_tok, n_tp),
        out_shape=(
            jax.ShapeDtypeStruct((m, outs), BF16),
            jax.ShapeDtypeStruct((m, win_rows), BF16),
            jax.ShapeDtypeStruct((m, win_cols), BF16),
        ),
        in_specs=[anywhere] * 4,
        out_specs=(vmem, vmem, vmem),
        scratch_shapes=[
            pltpu.VMEM((n_tok, rows, feats), BF16),
            pltpu.VMEM((nc, 2, feats, w), BF16),
            pltpu.VMEM((nc, w, outs), BF16),
            pltpu.VMEM((nc, 2, 2, m // 2, w), BF16),
            pltpu.VMEM((nc, 2, m // 2, w), BF16),
            pltpu.VMEM((nc, n_x, 2, b, w), BF16),
            pltpu.VMEM((nc, n_x, 2, b, w), BF16),
            pltpu.VMEM((nc, n_tp, b, w), BF16),
            pltpu.VMEM((m, outs), F32),
            pltpu.VMEM((n_tok, rows, outs), BF16),
            pltpu.VMEM((n_tok, rows, outs), BF16),
            pltpu.VMEM((n_tok, rows, outs), BF16),
            pltpu.VMEM((n_tok, rows, win_rows), BF16),
            pltpu.VMEM((n_tok, rows, win_cols), BF16),
            dma(()), dma((nc, 2)), dma((nc,)),
            dma((n_tok,)), dma((n_tok,)),
            dma((nc,)), dma((nc,)),
            dma((nc, n_x)), dma((nc, n_x)),
            dma((nc, n_x)), dma((nc, n_x)),
            dma((nc, n_x)), dma((nc, n_x)),
            dma((n_tok,)), dma((n_tok,)),
            dma((n_tok,)), dma((n_tok,)),
            dma((n_tp,)), dma(()),
            dma((n_tp,)), dma(()),
        ],
        compiler_params=pltpu.CompilerParams(
            collective_id=0, has_side_effects=True, vmem_limit_bytes=58 * 2**20
        ),
        cost_estimate=pl.CostEstimate(
            flops=4 * m * feats * half + 2 * m * half * outs,
            bytes_accessed=2 * (2 * feats * half + half * outs),
            transcendentals=0,
        ),
    )(inputs, gate_weight, up_weight, down_weight)


def shards(n_tok, n_tp, inputs, gate_weight, up_weight, down_weight):
    target, win_rows, win_cols = span(inputs, gate_weight, up_weight, down_weight, n_tok, n_tp)
    gram = jnp.dot(win_rows.T, win_cols, preferred_element_type=F32)
    cross = jnp.dot(win_rows.T, target, preferred_element_type=F32)
    return gram, cross


def solution(mesh):
    placed = (P(("grp", "tok"), "tp"), P("tp", "tok"), P("tp", "tok"), P("tok", "tp"))
    return jax.shard_map(
        functools.partial(shards, mesh.shape["tok"], mesh.shape["tp"]),
        mesh=mesh,
        in_specs=placed,
        out_specs=(P(("grp", "tok"), "tp"), P(("grp", "tok"), "tp")),
        check_vma=False,
    )
```

```python
import functools

import jax
import jax.numpy as jnp
from jax import lax
from jax.experimental import pallas as pl
from jax.experimental.pallas import tpu as pltpu
from jax.sharding import PartitionSpec as P

WIN = 4096
CHUNK = 1024
LAGS = (2, 4, 6, 8)
Z_LAG = 3
STAT_ROWS = 256
MESH = pl.DeviceIdType.MESH
F32 = jnp.float32
BF16 = jnp.bfloat16


def span_kernel(
    n_tok, n_tp,
    x_ref, gate_ref, up_ref, down_ref,
    tgt_ref, wrow_ref, wcol_ref,
    xg, wg, wd, part, r1, s1, r2, hid, acc, ts, tr, tg, wr, wc,
    ld_x, ld_w, ld_d, gs, gr, c1s, c1r, x1s, x1r, x2s, x2r, c2s, c2r,
    zs, zr, bs, br, wrs, wrr, wcs, wcr,
):
    t = lax.axis_index("tok")
    p = lax.axis_index("tp")
    core = lax.rem(p, 2)
    x = p // 2
    n_x = n_tp // 2
    nc, _, feats, w = wg.shape
    rows = xg.shape[1]
    m = n_tok * rows // 2
    b = m // n_tp
    sub = rows // 2
    ns = 2 * nc
    early = n_tok // 2
    shift = n_tok // 4
    place = lax.rem(t + n_tok - shift, n_tok)
    win_rows, win_cols = wr.shape[2], wc.shape[2]

    def tok_peer(k):
        return lax.rem(t + k, n_tok)

    def x_peer(k):
        return lax.rem(x + k, n_x)

    def remote(src, dst, ssem, rsem, **where):
        return pltpu.make_async_remote_copy(
            src_ref=src, dst_ref=dst, send_sem=ssem, recv_sem=rsem,
            device_id=where, device_id_type=MESH,
        )

    partner = p + 1 - 2 * core

    own_x = pltpu.make_async_copy(x_ref, xg.at[place], ld_x)
    own_x.start()

    def load_w(c, j):
        src = (gate_ref, up_ref)[j]
        cols = pl.ds(pl.multiple_of(c * w, w), w)
        return pltpu.make_async_copy(src.at[:, cols], wg.at[c, j], ld_w.at[c, j])

    def load_d(c):
        return pltpu.make_async_copy(
            down_ref.at[pl.ds(pl.multiple_of(c * w, w), w), :], wd.at[c], ld_d.at[c]
        )

    @pl.loop(0, nc)
    def _(c):
        load_w(c, 0).start()
        load_w(c, 1).start()

    @pl.loop(0, nc)
    def _(c):
        load_d(c).start()

    barrier = pltpu.get_barrier_semaphore()
    for k in range(1, n_tok):
        pl.semaphore_signal(barrier, inc=1, device_id={"tok": tok_peer(k)}, device_id_type=MESH)
    for k in range(1, n_tp):
        pl.semaphore_signal(barrier, inc=1, device_id={"tp": lax.rem(p + k, n_tp)}, device_id_type=MESH)
    pl.semaphore_wait(barrier, n_tok + n_tp - 2)

    def gather(k):
        to = tok_peer(k)
        return remote(x_ref, xg.at[place], gs.at[to], gr.at[place], tok=to)

    def gathered(at):
        return remote(x_ref, xg.at[at], gs.at[at], gr.at[at], tok=tok_peer(1))

    def send_tokens():
        for k in range(1, n_tok):
            gather(k).start()

    def await_tokens(first, last):
        for at in range(first, last):

            @pl.when(place != at)
            def _(at=at):
                gathered(at).wait_recv()

    @pl.when(place < early)
    def _():
        send_tokens()

    own_x.wait()
    await_tokens(0, early)

    @pl.when(place >= early)
    def _():
        send_tokens()

    def core_sum(c):
        return remote(part.at[c, 1 - core], r1.at[c], c1s.at[c], c1r.at[c], tp=partner)

    def x_sum(c, k):
        to = x_peer(k)
        return remote(s1.at[c, to], r2.at[c, x], x1s.at[c, to], x1r.at[c, x], tp=2 * to + core)

    def x_summed(c, k):
        src = x_peer(k)
        return remote(s1.at[c, src], r2.at[c, src], x1s.at[c, src], x1r.at[c, src], tp=2 * src + core)

    def x_hid(c, k):
        to = x_peer(k)
        mine = hid.at[c, core * n_x + x]
        return remote(mine, mine, x2s.at[c, to], x2r.at[c, x], tp=2 * to + core)

    def x_hidden(c, k):
        src = x_peer(k)
        theirs = hid.at[c, core * n_x + src]
        return remote(theirs, theirs, x2s.at[c, src], x2r.at[c, src], tp=2 * src + core)

    def core_hid(c, k):
        at = x_peer(k)
        block = hid.at[c, core * n_x + at]
        return remote(block, block, c2s.at[c, at], c2r.at[c, at], tp=partner)

    def core_hidden(c, k):
        at = x_peer(k)
        block = hid.at[c, (1 - core) * n_x + at]
        return remote(block, block, c2s.at[c, at], c2r.at[c, at], tp=partner)

    def z_sum(h, k):
        to = tok_peer(k)
        return remote(ts.at[h, to], tr.at[h, t], zs.at[h, to], zr.at[h, t], tok=to)

    def z_summed(h, k):
        src = tok_peer(k)
        return remote(ts.at[h, src], tr.at[h, src], zs.at[h, src], zr.at[h, src], tok=src)

    def z_all(h, k):
        to = tok_peer(k)
        return remote(tg.at[h, t], tg.at[h, t], bs.at[h, to], br.at[h, t], tok=to)

    def z_alled(h, k):
        src = tok_peer(k)
        return remote(tg.at[h, src], tg.at[h, src], bs.at[h, src], br.at[h, src], tok=src)

    def z_send(h):
        ts[h] = acc[h].astype(BF16).reshape(ts.shape[1:])
        for k in range(1, n_tok):
            z_sum(h, k).start()

    def z_reduce(h):
        total = acc[h, pl.ds(pl.multiple_of(t * sub, sub), sub), :]
        for k in range(1, n_tok):
            z_summed(h, k).wait_recv()
            total = total + tr[h, tok_peer(k)].astype(F32)
        tg[h, t] = total.astype(BF16)
        for k in range(1, n_tok):
            z_all(h, k).start()

    def col_copy(d):
        off = (d * win_cols) % feats
        return remote(xg.at[:, :, pl.ds(off, win_cols)], wc, wcs.at[d], wcr, tp=d)

    row_owner = (t * win_rows) // feats
    row_off = pl.multiple_of(lax.rem(t * win_rows, feats), win_rows)

    def row_copy(k):
        to = lax.rem(p + k, n_tp)
        return remote(xg.at[:, :, pl.ds(row_off, win_rows)], wr, wrs.at[k], wrr, tp=to)

    def send_window():
        for d in range(n_tp):
            owner = d * win_cols // feats

            @pl.when(p == owner)
            def _(d=d, owner=owner):
                if d == owner:
                    off = (d * win_cols) % feats
                    wc[...] = xg[:, :, off : off + win_cols]
                else:
                    col_copy(d).start()

        @pl.when(p == row_owner)
        def _():
            for k in range(1, n_tp):
                row_copy(k).start()
            wr[...] = xg[:, :, pl.ds(row_off, win_rows)]

    lag_sum, lag_act, lag_fwd, lag_down = LAGS
    steps = ns + lag_down
    acc[...] = jnp.zeros_like(acc)

    def step(s, carry):
        @pl.when(s == nc)
        def _():
            await_tokens(early, n_tok)

        @pl.when(s < nc)
        def _():
            load_w(s, 0).wait()
            load_w(s, 1).wait()

        @pl.when(s < ns)
        def _():
            c = s
            half, at = c // nc, lax.rem(c, nc)
            tokens = xg[pl.ds(half * early, early)].reshape(m, feats)
            for j in range(2):
                y = jnp.dot(tokens, wg[at, j], preferred_element_type=F32).astype(BF16)
                part[c, 0, j] = y[: m // 2]
                part[c, 1, j] = y[m // 2 :]
            core_sum(c).start()

        @pl.when((s >= lag_sum) & (s < ns + lag_sum))
        def _():
            c = s - lag_sum
            core_sum(c).wait_recv()
            both = part[c, core].astype(F32) + r1[c].astype(F32)
            both = both.astype(BF16)
            for at in range(n_x):
                s1[c, at] = both[:, at * b : (at + 1) * b]
            for k in range(1, n_x):
                x_sum(c, k).start()

        @pl.when((s >= lag_act) & (s < ns + lag_act))
        def _():
            c = s - lag_act
            for k in range(1, n_x):
                x_summed(c, k).wait_recv()
            both = s1[c, x].astype(F32)
            for k in range(1, n_x):
                both = both + r2[c, x_peer(k)].astype(F32)
            g, u = both[0], both[1]
            hid[c, core * n_x + x] = (g / (1.0 + jnp.exp(-g)) * u).astype(BF16)
            for k in range(1, n_x):
                x_hid(c, k).start()
            core_hid(c, 0).start()

        @pl.when(s == ns - 1 + lag_act)
        def _():
            send_window()

        @pl.when((s >= lag_fwd) & (s < ns + lag_fwd))
        def _():
            c = s - lag_fwd
            for k in range(1, n_x):
                x_hidden(c, k).wait_recv()
                core_hid(c, k).start()

        @pl.when(s >= lag_down)
        def _():
            c = s - lag_down
            for k in range(n_x):
                core_hidden(c, k).wait_recv()
            half, at = c // nc, lax.rem(c, nc)

            @pl.when(c < nc)
            def _():
                load_d(c).wait()

            acc[half] += jnp.dot(hid[c].reshape(m, w), wd[at], preferred_element_type=F32)

        @pl.when(s == nc - 1 + lag_down)
        def _():
            z_send(0)

        @pl.when(s == min(nc - 1 + lag_down + Z_LAG, steps - 1))
        def _():
            z_reduce(0)

        return carry

    lax.fori_loop(0, steps, step, 0)
    z_send(1)

    z_reduce(1)

    @pl.when((p * win_cols) // feats != p)
    def _():
        col_copy(0).wait_recv()

    @pl.when(p != row_owner)
    def _():
        row_copy(1).wait_recv()

    wrow_ref[...] = wr[...].reshape(wrow_ref.shape)
    wcol_ref[...] = wc[...].reshape(wcol_ref.shape)
    for h in range(2):
        for k in range(1, n_tok):
            z_alled(h, k).wait_recv()
    tgt_ref[...] = tg[...].reshape(tgt_ref.shape)

    @pl.loop(0, ns)
    def _(c):
        core_sum(c).wait_send()
        core_hid(c, 0).wait_send()
        for k in range(1, n_x):
            x_sum(c, k).wait_send()
            x_hid(c, k).wait_send()
            core_hid(c, k).wait_send()

    for k in range(1, n_tok):
        gather(k).wait_send()
        for h in range(2):
            z_sum(h, k).wait_send()
            z_all(h, k).wait_send()
    for d in range(n_tp):
        owner = d * win_cols // feats
        if d != owner:

            @pl.when(p == owner)
            def _(d=d):
                col_copy(d).wait_send()

    @pl.when(p == row_owner)
    def _():
        for k in range(1, n_tp):
            row_copy(k).wait_send()


def span(inputs, gate_weight, up_weight, down_weight, n_tok, n_tp):
    rows, feats = inputs.shape
    half = gate_weight.shape[1]
    outs = down_weight.shape[1]
    m = n_tok * rows // 2
    sub = rows // 2
    w = min(CHUNK, half)
    nc = half // w
    ns = 2 * nc
    n_x = n_tp // 2
    b = m // n_tp
    win_rows, win_cols = WIN // n_tok, WIN // n_tp
    dma = pltpu.SemaphoreType.DMA
    anywhere = pl.BlockSpec(memory_space=pl.ANY)
    vmem = pl.BlockSpec(memory_space=pltpu.VMEM)
    return pl.pallas_call(
        functools.partial(span_kernel, n_tok, n_tp),
        out_shape=(
            jax.ShapeDtypeStruct((2 * m, outs), BF16),
            jax.ShapeDtypeStruct((2 * m, win_rows), BF16),
            jax.ShapeDtypeStruct((2 * m, win_cols), BF16),
        ),
        in_specs=[anywhere] * 4,
        out_specs=(vmem, vmem, vmem),
        scratch_shapes=[
            pltpu.VMEM((n_tok, rows, feats), BF16),
            pltpu.VMEM((nc, 2, feats, w), BF16),
            pltpu.VMEM((nc, w, outs), BF16),
            pltpu.VMEM((ns, 2, 2, m // 2, w), BF16),
            pltpu.VMEM((ns, 2, m // 2, w), BF16),
            pltpu.VMEM((ns, n_x, 2, b, w), BF16),
            pltpu.VMEM((ns, n_x, 2, b, w), BF16),
            pltpu.VMEM((ns, n_tp, b, w), BF16),
            pltpu.VMEM((2, m, outs), F32),
            pltpu.VMEM((2, n_tok, sub, outs), BF16),
            pltpu.VMEM((2, n_tok, sub, outs), BF16),
            pltpu.VMEM((2, n_tok, sub, outs), BF16),
            pltpu.VMEM((n_tok, rows, win_rows), BF16),
            pltpu.VMEM((n_tok, rows, win_cols), BF16),
            dma(()), dma((nc, 2)), dma((nc,)),
            dma((n_tok,)), dma((n_tok,)),
            dma((ns,)), dma((ns,)),
            dma((ns, n_x)), dma((ns, n_x)),
            dma((ns, n_x)), dma((ns, n_x)),
            dma((ns, n_x)), dma((ns, n_x)),
            dma((2, n_tok)), dma((2, n_tok)),
            dma((2, n_tok)), dma((2, n_tok)),
            dma((n_tp,)), dma(()),
            dma((n_tp,)), dma(()),
        ],
        compiler_params=pltpu.CompilerParams(
            collective_id=0, has_side_effects=True, vmem_limit_bytes=58 * 2**20
        ),
        cost_estimate=pl.CostEstimate(
            flops=8 * m * feats * half + 4 * m * half * outs,
            bytes_accessed=2 * (2 * feats * half + half * outs),
            transcendentals=0,
        ),
    )(inputs, gate_weight, up_weight, down_weight)


def statistics_kernel(rows_ref, cols_ref, tgt_ref, gram_ref, cross_ref):
    turned = rows_ref[...].T
    gram_ref[...] = jnp.dot(turned, cols_ref[...], preferred_element_type=F32)
    cross_ref[...] = jnp.dot(turned, tgt_ref[...], preferred_element_type=F32)


def statistics(win_rows, win_cols, target):
    m, height = win_rows.shape
    width, outs = win_cols.shape[1], target.shape[1]
    tile = min(STAT_ROWS, height)
    whole = lambda n: pl.BlockSpec((m, n), lambda i: (0, 0))
    return pl.pallas_call(
        statistics_kernel,
        out_shape=(
            jax.ShapeDtypeStruct((height, width), F32),
            jax.ShapeDtypeStruct((height, outs), F32),
        ),
        grid=(height // tile,),
        in_specs=[pl.BlockSpec((m, tile), lambda i: (0, i)), whole(width), whole(outs)],
        out_specs=(
            pl.BlockSpec((tile, width), lambda i: (i, 0)),
            pl.BlockSpec((tile, outs), lambda i: (i, 0)),
        ),
        compiler_params=pltpu.CompilerParams(vmem_limit_bytes=32 * 2**20),
        cost_estimate=pl.CostEstimate(
            flops=2 * m * height * (width + outs),
            bytes_accessed=2 * m * (height + width + outs) + 4 * height * (width + outs),
            transcendentals=0,
        ),
    )(win_rows, win_cols, target)


def shards(n_tok, n_tp, inputs, gate_weight, up_weight, down_weight):
    target, win_rows, win_cols = span(inputs, gate_weight, up_weight, down_weight, n_tok, n_tp)
    return statistics(win_rows, win_cols, target)


def solution(mesh):
    placed = (P(("grp", "tok"), "tp"), P("tp", "tok"), P("tp", "tok"), P("tok", "tp"))
    return jax.shard_map(
        functools.partial(shards, mesh.shape["tok"], mesh.shape["tp"]),
        mesh=mesh,
        in_specs=placed,
        out_specs=(P(("grp", "tok"), "tp"), P(("grp", "tok"), "tp")),
        check_vma=False,
    )
```

```python
import functools

import jax
import jax.numpy as jnp
from jax import lax
from jax.experimental import pallas as pl
from jax.experimental.pallas import tpu as pltpu
from jax.sharding import PartitionSpec as P

WIN = 4096
CHUNK = 1024
LAGS = (1,2,3,4)
Z_LAG = 3
STAT_ROWS = 256
MESH = pl.DeviceIdType.MESH
F32 = jnp.float32
BF16 = jnp.bfloat16


def span_kernel(
    n_tok, n_tp,
    x_ref, gate_ref, up_ref, down_ref,
    tgt_ref, wrow_ref, wcol_ref,
    xg, wg, wd, part, r1, s1, r2, hid, acc, ts, tr, tg, wr, wc,
    ld_x, ld_w, ld_d, gs, gr, c1s, c1r, x1s, x1r, x2s, x2r, c2s, c2r,
    zs, zr, bs, br, wrs, wrr, wcs, wcr,
):
    t = lax.axis_index("tok")
    p = lax.axis_index("tp")
    core = lax.rem(p, 2)
    x = p // 2
    n_x = n_tp // 2
    nc, _, feats, w = wg.shape
    rows = xg.shape[1]
    m = n_tok * rows // 2
    b = m // n_tp
    sub = rows // 2
    ns = 2 * nc
    early = n_tok // 2
    shift = n_tok // 4
    place = lax.rem(t + n_tok - shift, n_tok)
    win_rows, win_cols = wr.shape[2], wc.shape[2]

    def tok_peer(k):
        return lax.rem(t + k, n_tok)

    def x_peer(k):
        return lax.rem(x + k, n_x)

    def remote(src, dst, ssem, rsem, **where):
        return pltpu.make_async_remote_copy(
            src_ref=src, dst_ref=dst, send_sem=ssem, recv_sem=rsem,
            device_id=where, device_id_type=MESH,
        )

    partner = p + 1 - 2 * core

    own_x = pltpu.make_async_copy(x_ref, xg.at[place], ld_x)
    own_x.start()

    def load_w(c, j):
        src = (gate_ref, up_ref)[j]
        cols = pl.ds(pl.multiple_of(c * w, w), w)
        return pltpu.make_async_copy(src.at[:, cols], wg.at[c, j], ld_w.at[c, j])

    def load_d(c):
        return pltpu.make_async_copy(
            down_ref.at[pl.ds(pl.multiple_of(c * w, w), w), :], wd.at[c], ld_d.at[c]
        )

    @pl.loop(0, nc)
    def _(c):
        load_w(c, 0).start()
        load_w(c, 1).start()

    @pl.loop(0, nc)
    def _(c):
        load_d(c).start()

    barrier = pltpu.get_barrier_semaphore()
    for k in range(1, n_tok):
        pl.semaphore_signal(barrier, inc=1, device_id={"tok": tok_peer(k)}, device_id_type=MESH)
    for k in range(1, n_tp):
        pl.semaphore_signal(barrier, inc=1, device_id={"tp": lax.rem(p + k, n_tp)}, device_id_type=MESH)
    pl.semaphore_wait(barrier, n_tok + n_tp - 2)

    def gather(k):
        to = tok_peer(k)
        return remote(x_ref, xg.at[place], gs.at[to], gr.at[place], tok=to)

    def gathered(at):
        return remote(x_ref, xg.at[at], gs.at[at], gr.at[at], tok=tok_peer(1))

    def send_tokens():
        for k in range(1, n_tok):
            gather(k).start()

    def await_tokens(first, last):
        for at in range(first, last):

            @pl.when(place != at)
            def _(at=at):
                gathered(at).wait_recv()

    @pl.when(place < early)
    def _():
        send_tokens()

    own_x.wait()
    await_tokens(0, early)

    @pl.when(place >= early)
    def _():
        send_tokens()

    def core_sum(c):
        return remote(part.at[c, 1 - core], r1.at[c], c1s.at[c], c1r.at[c], tp=partner)

    def x_sum(c, k):
        to = x_peer(k)
        return remote(s1.at[c, to], r2.at[c, x], x1s.at[c, to], x1r.at[c, x], tp=2 * to + core)

    def x_summed(c, k):
        src = x_peer(k)
        return remote(s1.at[c, src], r2.at[c, src], x1s.at[c, src], x1r.at[c, src], tp=2 * src + core)

    def x_hid(c, k):
        to = x_peer(k)
        mine = hid.at[c, core * n_x + x]
        return remote(mine, mine, x2s.at[c, to], x2r.at[c, x], tp=2 * to + core)

    def x_hidden(c, k):
        src = x_peer(k)
        theirs = hid.at[c, core * n_x + src]
        return remote(theirs, theirs, x2s.at[c, src], x2r.at[c, src], tp=2 * src + core)

    def core_hid(c, k):
        at = x_peer(k)
        block = hid.at[c, core * n_x + at]
        return remote(block, block, c2s.at[c, at], c2r.at[c, at], tp=partner)

    def core_hidden(c, k):
        at = x_peer(k)
        block = hid.at[c, (1 - core) * n_x + at]
        return remote(block, block, c2s.at[c, at], c2r.at[c, at], tp=partner)

    def z_sum(h, k):
        to = tok_peer(k)
        return remote(ts.at[h, to], tr.at[h, t], zs.at[h, to], zr.at[h, t], tok=to)

    def z_summed(h, k):
        src = tok_peer(k)
        return remote(ts.at[h, src], tr.at[h, src], zs.at[h, src], zr.at[h, src], tok=src)

    def z_all(h, k):
        to = tok_peer(k)
        return remote(tg.at[h, t], tg.at[h, t], bs.at[h, to], br.at[h, t], tok=to)

    def z_alled(h, k):
        src = tok_peer(k)
        return remote(tg.at[h, src], tg.at[h, src], bs.at[h, src], br.at[h, src], tok=src)

    def z_send(h):
        ts[h] = acc[h].astype(BF16).reshape(ts.shape[1:])
        for k in range(1, n_tok):
            z_sum(h, k).start()

    def z_reduce(h):
        total = acc[h, pl.ds(pl.multiple_of(t * sub, sub), sub), :]
        for k in range(1, n_tok):
            z_summed(h, k).wait_recv()
            total = total + tr[h, tok_peer(k)].astype(F32)
        tg[h, t] = total.astype(BF16)
        for k in range(1, n_tok):
            z_all(h, k).start()

    def col_copy(d):
        off = (d * win_cols) % feats
        return remote(xg.at[:, :, pl.ds(off, win_cols)], wc, wcs.at[d], wcr, tp=d)

    row_owner = (t * win_rows) // feats
    row_off = pl.multiple_of(lax.rem(t * win_rows, feats), win_rows)

    def row_copy(k):
        to = lax.rem(p + k, n_tp)
        return remote(xg.at[:, :, pl.ds(row_off, win_rows)], wr, wrs.at[k], wrr, tp=to)

    def send_window():
        for d in range(n_tp):
            owner = d * win_cols // feats

            @pl.when(p == owner)
            def _(d=d, owner=owner):
                if d == owner:
                    off = (d * win_cols) % feats
                    wc[...] = xg[:, :, off : off + win_cols]
                else:
                    col_copy(d).start()

        @pl.when(p == row_owner)
        def _():
            for k in range(1, n_tp):
                row_copy(k).start()
            wr[...] = xg[:, :, pl.ds(row_off, win_rows)]

    lag_sum, lag_act, lag_fwd, lag_down = LAGS
    steps = ns + lag_down
    acc[...] = jnp.zeros_like(acc)

    def step(s, carry):
        @pl.when(s == nc)
        def _():
            await_tokens(early, n_tok)

        @pl.when(s < nc)
        def _():
            load_w(s, 0).wait()
            load_w(s, 1).wait()

        @pl.when(s < ns)
        def _():
            c = s
            half, at = c // nc, lax.rem(c, nc)
            tokens = xg[pl.ds(half * early, early)].reshape(m, feats)
            for j in range(2):
                y = jnp.dot(tokens, wg[at, j], preferred_element_type=F32).astype(BF16)
                part[c, 0, j] = y[: m // 2]
                part[c, 1, j] = y[m // 2 :]
            core_sum(c).start()

        @pl.when((s >= lag_sum) & (s < ns + lag_sum))
        def _():
            c = s - lag_sum
            core_sum(c).wait_recv()
            both = part[c, core].astype(F32) + r1[c].astype(F32)
            both = both.astype(BF16)
            for at in range(n_x):
                s1[c, at] = both[:, at * b : (at + 1) * b]
            for k in range(1, n_x):
                x_sum(c, k).start()

        @pl.when((s >= lag_act) & (s < ns + lag_act))
        def _():
            c = s - lag_act
            for k in range(1, n_x):
                x_summed(c, k).wait_recv()
            both = s1[c, x].astype(F32)
            for k in range(1, n_x):
                both = both + r2[c, x_peer(k)].astype(F32)
            g, u = both[0], both[1]
            hid[c, core * n_x + x] = (g / (1.0 + jnp.exp(-g)) * u).astype(BF16)
            for k in range(1, n_x):
                x_hid(c, k).start()
            core_hid(c, 0).start()

        @pl.when(s == ns - 1 + lag_act)
        def _():
            send_window()

        @pl.when((s >= lag_fwd) & (s < ns + lag_fwd))
        def _():
            c = s - lag_fwd
            for k in range(1, n_x):
                x_hidden(c, k).wait_recv()
                core_hid(c, k).start()

        @pl.when(s >= lag_down)
        def _():
            c = s - lag_down
            for k in range(n_x):
                core_hidden(c, k).wait_recv()
            half, at = c // nc, lax.rem(c, nc)

            @pl.when(c < nc)
            def _():
                load_d(c).wait()

            acc[half] += jnp.dot(hid[c].reshape(m, w), wd[at], preferred_element_type=F32)

        @pl.when(s == nc - 1 + lag_down)
        def _():
            z_send(0)

        @pl.when(s == min(nc - 1 + lag_down + Z_LAG, steps - 1))
        def _():
            z_reduce(0)

        return carry

    lax.fori_loop(0, steps, step, 0)
    z_send(1)

    z_reduce(1)

    @pl.when((p * win_cols) // feats != p)
    def _():
        col_copy(0).wait_recv()

    @pl.when(p != row_owner)
    def _():
        row_copy(1).wait_recv()

    wrow_ref[...] = wr[...].reshape(wrow_ref.shape)
    wcol_ref[...] = wc[...].reshape(wcol_ref.shape)
    for h in range(2):
        for k in range(1, n_tok):
            z_alled(h, k).wait_recv()
    tgt_ref[...] = tg[...].reshape(tgt_ref.shape)

    @pl.loop(0, ns)
    def _(c):
        core_sum(c).wait_send()
        core_hid(c, 0).wait_send()
        for k in range(1, n_x):
            x_sum(c, k).wait_send()
            x_hid(c, k).wait_send()
            core_hid(c, k).wait_send()

    for k in range(1, n_tok):
        gather(k).wait_send()
        for h in range(2):
            z_sum(h, k).wait_send()
            z_all(h, k).wait_send()
    for d in range(n_tp):
        owner = d * win_cols // feats
        if d != owner:

            @pl.when(p == owner)
            def _(d=d):
                col_copy(d).wait_send()

    @pl.when(p == row_owner)
    def _():
        for k in range(1, n_tp):
            row_copy(k).wait_send()


def span(inputs, gate_weight, up_weight, down_weight, n_tok, n_tp):
    rows, feats = inputs.shape
    half = gate_weight.shape[1]
    outs = down_weight.shape[1]
    m = n_tok * rows // 2
    sub = rows // 2
    w = min(CHUNK, half)
    nc = half // w
    ns = 2 * nc
    n_x = n_tp // 2
    b = m // n_tp
    win_rows, win_cols = WIN // n_tok, WIN // n_tp
    dma = pltpu.SemaphoreType.DMA
    anywhere = pl.BlockSpec(memory_space=pl.ANY)
    vmem = pl.BlockSpec(memory_space=pltpu.VMEM)
    return pl.pallas_call(
        functools.partial(span_kernel, n_tok, n_tp),
        out_shape=(
            jax.ShapeDtypeStruct((2 * m, outs), BF16),
            jax.ShapeDtypeStruct((2 * m, win_rows), BF16),
            jax.ShapeDtypeStruct((2 * m, win_cols), BF16),
        ),
        in_specs=[anywhere] * 4,
        out_specs=(vmem, vmem, vmem),
        scratch_shapes=[
            pltpu.VMEM((n_tok, rows, feats), BF16),
            pltpu.VMEM((nc, 2, feats, w), BF16),
            pltpu.VMEM((nc, w, outs), BF16),
            pltpu.VMEM((ns, 2, 2, m // 2, w), BF16),
            pltpu.VMEM((ns, 2, m // 2, w), BF16),
            pltpu.VMEM((ns, n_x, 2, b, w), BF16),
            pltpu.VMEM((ns, n_x, 2, b, w), BF16),
            pltpu.VMEM((ns, n_tp, b, w), BF16),
            pltpu.VMEM((2, m, outs), F32),
            pltpu.VMEM((2, n_tok, sub, outs), BF16),
            pltpu.VMEM((2, n_tok, sub, outs), BF16),
            pltpu.VMEM((2, n_tok, sub, outs), BF16),
            pltpu.VMEM((n_tok, rows, win_rows), BF16),
            pltpu.VMEM((n_tok, rows, win_cols), BF16),
            dma(()), dma((nc, 2)), dma((nc,)),
            dma((n_tok,)), dma((n_tok,)),
            dma((ns,)), dma((ns,)),
            dma((ns, n_x)), dma((ns, n_x)),
            dma((ns, n_x)), dma((ns, n_x)),
            dma((ns, n_x)), dma((ns, n_x)),
            dma((2, n_tok)), dma((2, n_tok)),
            dma((2, n_tok)), dma((2, n_tok)),
            dma((n_tp,)), dma(()),
            dma((n_tp,)), dma(()),
        ],
        compiler_params=pltpu.CompilerParams(
            collective_id=0, has_side_effects=True, vmem_limit_bytes=58 * 2**20
        ),
        cost_estimate=pl.CostEstimate(
            flops=8 * m * feats * half + 4 * m * half * outs,
            bytes_accessed=2 * (2 * feats * half + half * outs),
            transcendentals=0,
        ),
    )(inputs, gate_weight, up_weight, down_weight)


def statistics_kernel(rows_ref, cols_ref, tgt_ref, gram_ref, cross_ref):
    turned = rows_ref[...].T
    gram_ref[...] = jnp.dot(turned, cols_ref[...], preferred_element_type=F32)
    cross_ref[...] = jnp.dot(turned, tgt_ref[...], preferred_element_type=F32)


def statistics(win_rows, win_cols, target):
    m, height = win_rows.shape
    width, outs = win_cols.shape[1], target.shape[1]
    tile = min(STAT_ROWS, height)
    whole = lambda n: pl.BlockSpec((m, n), lambda i: (0, 0))
    return pl.pallas_call(
        statistics_kernel,
        out_shape=(
            jax.ShapeDtypeStruct((height, width), F32),
            jax.ShapeDtypeStruct((height, outs), F32),
        ),
        grid=(height // tile,),
        in_specs=[pl.BlockSpec((m, tile), lambda i: (0, i)), whole(width), whole(outs)],
        out_specs=(
            pl.BlockSpec((tile, width), lambda i: (i, 0)),
            pl.BlockSpec((tile, outs), lambda i: (i, 0)),
        ),
        compiler_params=pltpu.CompilerParams(vmem_limit_bytes=58 * 2**20),
        cost_estimate=pl.CostEstimate(
            flops=2 * m * height * (width + outs),
            bytes_accessed=2 * m * (height + width + outs) + 4 * height * (width + outs),
            transcendentals=0,
        ),
    )(win_rows, win_cols, target)


def shards(n_tok, n_tp, inputs, gate_weight, up_weight, down_weight):
    target, win_rows, win_cols = span(inputs, gate_weight, up_weight, down_weight, n_tok, n_tp)
    return statistics(win_rows, win_cols, target)


def solution(mesh):
    placed = (P(("grp", "tok"), "tp"), P("tp", "tok"), P("tp", "tok"), P("tok", "tp"))
    return jax.shard_map(
        functools.partial(shards, mesh.shape["tok"], mesh.shape["tp"]),
        mesh=mesh,
        in_specs=placed,
        out_specs=(P(("grp", "tok"), "tp"), P(("grp", "tok"), "tp")),
        check_vma=False,
    )
```

```python
import functools

import jax
import jax.numpy as jnp
from jax import lax
from jax.experimental import pallas as pl
from jax.experimental.pallas import tpu as pltpu
from jax.sharding import PartitionSpec as P

WIN = 4096
CHUNK = 1024
LAGS = (1,2,3,4)
Z_LAG = 3
STAT_ROWS = 128
MESH = pl.DeviceIdType.MESH
F32 = jnp.float32
BF16 = jnp.bfloat16


def span_kernel(
    n_tok, n_tp,
    x_ref, gate_ref, up_ref, down_ref,
    tgt_ref, wrow_ref, wcol_ref,
    xg, wg, wd, part, r1, s1, r2, hid, acc, ts, tr, tg, wr, wc,
    ld_x, ld_w, ld_d, gs, gr, c1s, c1r, x1s, x1r, x2s, x2r, c2s, c2r,
    zs, zr, bs, br, wrs, wrr, wcs, wcr,
):
    t = lax.axis_index("tok")
    p = lax.axis_index("tp")
    core = lax.rem(p, 2)
    x = p // 2
    n_x = n_tp // 2
    nc, _, feats, w = wg.shape
    rows = xg.shape[1]
    m = n_tok * rows // 2
    b = m // n_tp
    sub = rows // 2
    ns = 2 * nc
    early = n_tok // 2
    shift = n_tok // 4
    place = lax.rem(t + n_tok - shift, n_tok)
    win_rows, win_cols = wr.shape[2], wc.shape[2]

    def tok_peer(k):
        return lax.rem(t + k, n_tok)

    def x_peer(k):
        return lax.rem(x + k, n_x)

    def remote(src, dst, ssem, rsem, **where):
        return pltpu.make_async_remote_copy(
            src_ref=src, dst_ref=dst, send_sem=ssem, recv_sem=rsem,
            device_id=where, device_id_type=MESH,
        )

    partner = p + 1 - 2 * core

    own_x = pltpu.make_async_copy(x_ref, xg.at[place], ld_x)
    own_x.start()

    def load_w(c, j):
        src = (gate_ref, up_ref)[j]
        cols = pl.ds(pl.multiple_of(c * w, w), w)
        return pltpu.make_async_copy(src.at[:, cols], wg.at[c, j], ld_w.at[c, j])

    def load_d(c):
        return pltpu.make_async_copy(
            down_ref.at[pl.ds(pl.multiple_of(c * w, w), w), :], wd.at[c], ld_d.at[c]
        )

    @pl.loop(0, nc)
    def _(c):
        load_w(c, 0).start()
        load_w(c, 1).start()

    @pl.loop(0, nc)
    def _(c):
        load_d(c).start()

    barrier = pltpu.get_barrier_semaphore()
    for k in range(1, n_tok):
        pl.semaphore_signal(barrier, inc=1, device_id={"tok": tok_peer(k)}, device_id_type=MESH)
    for k in range(1, n_tp):
        pl.semaphore_signal(barrier, inc=1, device_id={"tp": lax.rem(p + k, n_tp)}, device_id_type=MESH)
    pl.semaphore_wait(barrier, n_tok + n_tp - 2)

    def gather(k):
        to = tok_peer(k)
        return remote(x_ref, xg.at[place], gs.at[to], gr.at[place], tok=to)

    def gathered(at):
        return remote(x_ref, xg.at[at], gs.at[at], gr.at[at], tok=tok_peer(1))

    def send_tokens():
        for k in range(1, n_tok):
            gather(k).start()

    def await_tokens(first, last):
        for at in range(first, last):

            @pl.when(place != at)
            def _(at=at):
                gathered(at).wait_recv()

    @pl.when(place < early)
    def _():
        send_tokens()

    own_x.wait()
    await_tokens(0, early)

    @pl.when(place >= early)
    def _():
        send_tokens()

    def core_sum(c):
        return remote(part.at[c, 1 - core], r1.at[c], c1s.at[c], c1r.at[c], tp=partner)

    def x_sum(c, k):
        to = x_peer(k)
        return remote(s1.at[c, to], r2.at[c, x], x1s.at[c, to], x1r.at[c, x], tp=2 * to + core)

    def x_summed(c, k):
        src = x_peer(k)
        return remote(s1.at[c, src], r2.at[c, src], x1s.at[c, src], x1r.at[c, src], tp=2 * src + core)

    def x_hid(c, k):
        to = x_peer(k)
        mine = hid.at[c, core * n_x + x]
        return remote(mine, mine, x2s.at[c, to], x2r.at[c, x], tp=2 * to + core)

    def x_hidden(c, k):
        src = x_peer(k)
        theirs = hid.at[c, core * n_x + src]
        return remote(theirs, theirs, x2s.at[c, src], x2r.at[c, src], tp=2 * src + core)

    def core_hid(c, k):
        at = x_peer(k)
        block = hid.at[c, core * n_x + at]
        return remote(block, block, c2s.at[c, at], c2r.at[c, at], tp=partner)

    def core_hidden(c, k):
        at = x_peer(k)
        block = hid.at[c, (1 - core) * n_x + at]
        return remote(block, block, c2s.at[c, at], c2r.at[c, at], tp=partner)

    def z_sum(h, k):
        to = tok_peer(k)
        return remote(ts.at[h, to], tr.at[h, t], zs.at[h, to], zr.at[h, t], tok=to)

    def z_summed(h, k):
        src = tok_peer(k)
        return remote(ts.at[h, src], tr.at[h, src], zs.at[h, src], zr.at[h, src], tok=src)

    def z_all(h, k):
        to = tok_peer(k)
        return remote(tg.at[h, t], tg.at[h, t], bs.at[h, to], br.at[h, t], tok=to)

    def z_alled(h, k):
        src = tok_peer(k)
        return remote(tg.at[h, src], tg.at[h, src], bs.at[h, src], br.at[h, src], tok=src)

    def z_send(h):
        ts[h] = acc[h].astype(BF16).reshape(ts.shape[1:])
        for k in range(1, n_tok):
            z_sum(h, k).start()

    def z_reduce(h):
        total = acc[h, pl.ds(pl.multiple_of(t * sub, sub), sub), :]
        for k in range(1, n_tok):
            z_summed(h, k).wait_recv()
            total = total + tr[h, tok_peer(k)].astype(F32)
        tg[h, t] = total.astype(BF16)
        for k in range(1, n_tok):
            z_all(h, k).start()

    def col_copy(d):
        off = (d * win_cols) % feats
        return remote(xg.at[:, :, pl.ds(off, win_cols)], wc, wcs.at[d], wcr, tp=d)

    row_owner = (t * win_rows) // feats
    row_off = pl.multiple_of(lax.rem(t * win_rows, feats), win_rows)

    def row_copy(k):
        to = lax.rem(p + k, n_tp)
        return remote(xg.at[:, :, pl.ds(row_off, win_rows)], wr, wrs.at[k], wrr, tp=to)

    def send_window():
        for d in range(n_tp):
            owner = d * win_cols // feats

            @pl.when(p == owner)
            def _(d=d, owner=owner):
                if d == owner:
                    off = (d * win_cols) % feats
                    wc[...] = xg[:, :, off : off + win_cols]
                else:
                    col_copy(d).start()

        @pl.when(p == row_owner)
        def _():
            for k in range(1, n_tp):
                row_copy(k).start()
            wr[...] = xg[:, :, pl.ds(row_off, win_rows)]

    lag_sum, lag_act, lag_fwd, lag_down = LAGS
    steps = ns + lag_down
    acc[...] = jnp.zeros_like(acc)

    def step(s, carry):
        @pl.when(s == nc)
        def _():
            await_tokens(early, n_tok)

        @pl.when(s < nc)
        def _():
            load_w(s, 0).wait()
            load_w(s, 1).wait()

        @pl.when(s < ns)
        def _():
            c = s
            half, at = c // nc, lax.rem(c, nc)
            tokens = xg[pl.ds(half * early, early)].reshape(m, feats)
            for j in range(2):
                y = jnp.dot(tokens, wg[at, j], preferred_element_type=F32).astype(BF16)
                part[c, 0, j] = y[: m // 2]
                part[c, 1, j] = y[m // 2 :]
            core_sum(c).start()

        @pl.when((s >= lag_sum) & (s < ns + lag_sum))
        def _():
            c = s - lag_sum
            core_sum(c).wait_recv()
            both = part[c, core].astype(F32) + r1[c].astype(F32)
            both = both.astype(BF16)
            for at in range(n_x):
                s1[c, at] = both[:, at * b : (at + 1) * b]
            for k in range(1, n_x):
                x_sum(c, k).start()

        @pl.when((s >= lag_act) & (s < ns + lag_act))
        def _():
            c = s - lag_act
            for k in range(1, n_x):
                x_summed(c, k).wait_recv()
            both = s1[c, x].astype(F32)
            for k in range(1, n_x):
                both = both + r2[c, x_peer(k)].astype(F32)
            g, u = both[0], both[1]
            hid[c, core * n_x + x] = (g / (1.0 + jnp.exp(-g)) * u).astype(BF16)
            for k in range(1, n_x):
                x_hid(c, k).start()
            core_hid(c, 0).start()

        @pl.when(s == ns - 1 + lag_act)
        def _():
            send_window()

        @pl.when((s >= lag_fwd) & (s < ns + lag_fwd))
        def _():
            c = s - lag_fwd
            for k in range(1, n_x):
                x_hidden(c, k).wait_recv()
                core_hid(c, k).start()

        @pl.when(s >= lag_down)
        def _():
            c = s - lag_down
            for k in range(n_x):
                core_hidden(c, k).wait_recv()
            half, at = c // nc, lax.rem(c, nc)

            @pl.when(c < nc)
            def _():
                load_d(c).wait()

            acc[half] += jnp.dot(hid[c].reshape(m, w), wd[at], preferred_element_type=F32)

        @pl.when(s == nc - 1 + lag_down)
        def _():
            z_send(0)

        @pl.when(s == min(nc - 1 + lag_down + Z_LAG, steps - 1))
        def _():
            z_reduce(0)

        return carry

    lax.fori_loop(0, steps, step, 0)
    z_send(1)

    z_reduce(1)

    @pl.when((p * win_cols) // feats != p)
    def _():
        col_copy(0).wait_recv()

    @pl.when(p != row_owner)
    def _():
        row_copy(1).wait_recv()

    wrow_ref[...] = wr[...].reshape(wrow_ref.shape)
    wcol_ref[...] = wc[...].reshape(wcol_ref.shape)
    for h in range(2):
        for k in range(1, n_tok):
            z_alled(h, k).wait_recv()
    tgt_ref[...] = tg[...].reshape(tgt_ref.shape)

    @pl.loop(0, ns)
    def _(c):
        core_sum(c).wait_send()
        core_hid(c, 0).wait_send()
        for k in range(1, n_x):
            x_sum(c, k).wait_send()
            x_hid(c, k).wait_send()
            core_hid(c, k).wait_send()

    for k in range(1, n_tok):
        gather(k).wait_send()
        for h in range(2):
            z_sum(h, k).wait_send()
            z_all(h, k).wait_send()
    for d in range(n_tp):
        owner = d * win_cols // feats
        if d != owner:

            @pl.when(p == owner)
            def _(d=d):
                col_copy(d).wait_send()

    @pl.when(p == row_owner)
    def _():
        for k in range(1, n_tp):
            row_copy(k).wait_send()


def span(inputs, gate_weight, up_weight, down_weight, n_tok, n_tp):
    rows, feats = inputs.shape
    half = gate_weight.shape[1]
    outs = down_weight.shape[1]
    m = n_tok * rows // 2
    sub = rows // 2
    w = min(CHUNK, half)
    nc = half // w
    ns = 2 * nc
    n_x = n_tp // 2
    b = m // n_tp
    win_rows, win_cols = WIN // n_tok, WIN // n_tp
    dma = pltpu.SemaphoreType.DMA
    anywhere = pl.BlockSpec(memory_space=pl.ANY)
    vmem = pl.BlockSpec(memory_space=pltpu.VMEM)
    return pl.pallas_call(
        functools.partial(span_kernel, n_tok, n_tp),
        out_shape=(
            jax.ShapeDtypeStruct((2 * m, outs), BF16),
            jax.ShapeDtypeStruct((2 * m, win_rows), BF16),
            jax.ShapeDtypeStruct((2 * m, win_cols), BF16),
        ),
        in_specs=[anywhere] * 4,
        out_specs=(vmem, vmem, vmem),
        scratch_shapes=[
            pltpu.VMEM((n_tok, rows, feats), BF16),
            pltpu.VMEM((nc, 2, feats, w), BF16),
            pltpu.VMEM((nc, w, outs), BF16),
            pltpu.VMEM((ns, 2, 2, m // 2, w), BF16),
            pltpu.VMEM((ns, 2, m // 2, w), BF16),
            pltpu.VMEM((ns, n_x, 2, b, w), BF16),
            pltpu.VMEM((ns, n_x, 2, b, w), BF16),
            pltpu.VMEM((ns, n_tp, b, w), BF16),
            pltpu.VMEM((2, m, outs), F32),
            pltpu.VMEM((2, n_tok, sub, outs), BF16),
            pltpu.VMEM((2, n_tok, sub, outs), BF16),
            pltpu.VMEM((2, n_tok, sub, outs), BF16),
            pltpu.VMEM((n_tok, rows, win_rows), BF16),
            pltpu.VMEM((n_tok, rows, win_cols), BF16),
            dma(()), dma((nc, 2)), dma((nc,)),
            dma((n_tok,)), dma((n_tok,)),
            dma((ns,)), dma((ns,)),
            dma((ns, n_x)), dma((ns, n_x)),
            dma((ns, n_x)), dma((ns, n_x)),
            dma((ns, n_x)), dma((ns, n_x)),
            dma((2, n_tok)), dma((2, n_tok)),
            dma((2, n_tok)), dma((2, n_tok)),
            dma((n_tp,)), dma(()),
            dma((n_tp,)), dma(()),
        ],
        compiler_params=pltpu.CompilerParams(
            collective_id=0, has_side_effects=True, vmem_limit_bytes=58 * 2**20
        ),
        cost_estimate=pl.CostEstimate(
            flops=8 * m * feats * half + 4 * m * half * outs,
            bytes_accessed=2 * (2 * feats * half + half * outs),
            transcendentals=0,
        ),
    )(inputs, gate_weight, up_weight, down_weight)


def statistics_kernel(rows_ref, cols_ref, tgt_ref, gram_ref, cross_ref):
    turned = rows_ref[...].T
    gram_ref[...] = jnp.dot(turned, cols_ref[...], preferred_element_type=F32)
    cross_ref[...] = jnp.dot(turned, tgt_ref[...], preferred_element_type=F32)


def statistics(win_rows, win_cols, target):
    m, height = win_rows.shape
    width, outs = win_cols.shape[1], target.shape[1]
    tile = min(STAT_ROWS, height)
    whole = lambda n: pl.BlockSpec((m, n), lambda i: (0, 0))
    return pl.pallas_call(
        statistics_kernel,
        out_shape=(
            jax.ShapeDtypeStruct((height, width), F32),
            jax.ShapeDtypeStruct((height, outs), F32),
        ),
        grid=(height // tile,),
        in_specs=[pl.BlockSpec((m, tile), lambda i: (0, i)), whole(width), whole(outs)],
        out_specs=(
            pl.BlockSpec((tile, width), lambda i: (i, 0)),
            pl.BlockSpec((tile, outs), lambda i: (i, 0)),
        ),
        compiler_params=pltpu.CompilerParams(vmem_limit_bytes=58 * 2**20),
        cost_estimate=pl.CostEstimate(
            flops=2 * m * height * (width + outs),
            bytes_accessed=2 * m * (height + width + outs) + 4 * height * (width + outs),
            transcendentals=0,
        ),
    )(win_rows, win_cols, target)


def shards(n_tok, n_tp, inputs, gate_weight, up_weight, down_weight):
    target, win_rows, win_cols = span(inputs, gate_weight, up_weight, down_weight, n_tok, n_tp)
    return statistics(win_rows, win_cols, target)


def solution(mesh):
    placed = (P(("grp", "tok"), "tp"), P("tp", "tok"), P("tp", "tok"), P("tok", "tp"))
    return jax.shard_map(
        functools.partial(shards, mesh.shape["tok"], mesh.shape["tp"]),
        mesh=mesh,
        in_specs=placed,
        out_specs=(P(("grp", "tok"), "tp"), P(("grp", "tok"), "tp")),
        check_vma=False,
    )
```
